256 devices in a mesh: dp: 4 (over y), fsdp: 64 (over x, z, core).
Axes of the slice: x: 4, y: 4, z: 8, core: 2. Of those that a mesh axis runs over, the one named last changes fastest.
Arguments:
- grads: bfloat16 [4, 256, 512, 512], P('dp', None, 'fsdp'), may hold values from -1.25 to 1.25
- stats_left: float32 [512, 512, 512], P(('dp', 'fsdp'))
- stats_right: float32 [512, 512, 512], P(('dp', 'fsdp'))
- precond_left: bfloat16 [512, 512, 512], P(('dp', 'fsdp'))
- precond_right: bfloat16 [512, 512, 512], P(('dp', 'fsdp'))
- owner_table: int32 [256], replicated, may hold values from 0 to 127, as said below
- block_counts: int32 [4, 64], P('dp', 'fsdp'), may hold values from 0 to 2, as said below
Outputs:
- new_left: float32 [512, 512, 512], P(('dp', 'fsdp'))
- new_right: float32 [512, 512, 512], P(('dp', 'fsdp'))
- update: bfloat16 [256, 512, 512], P(None, 'fsdp')
The draws below stay inside these ranges and needn't reach their ends.
Inputs may be any that keep to these rules, and one draw needn't show every extreme that they name: `owner_table`: within each group of 64 consecutive blocks no two blocks share an entry; the slots that a group uses on one device are 0 to one less than that device's count; in each group max(1, 8) devices own 2 blocks each, and no other device owns more than 1. block_counts[d, o] is the number of blocks of group d whose entry names device o.
All inputs are finite; a program needn't handle non-finite values.
Results may differ from the reference program's by a relative error of at most 0.017.
Values may be sent and summed in bfloat16 or wider, within the bound.
No kernel may reach another device: no remote copies, remote signals or barrier semaphores. Data moves between devices by JAX's collectives and lax.ppermute only.
A program may use at most 64 MiB of HBM per device.

```python
import math
import jax
import jax.numpy as jnp
from jax import lax

B = 512
CAP = 2
NBLK = 256
GBLK = 64
SLOTS = 512
N_DP = 4
N_FSDP = 64


def owner_layout(key):
    group_blocks = NBLK // N_DP
    full_count = max(1, N_FSDP // 8)
    rest_start = full_count * CAP
    others = N_FSDP - full_count
    positions = jnp.arange(group_blocks, dtype=jnp.int32)
    in_full = positions < rest_start
    rest_pos = jnp.maximum(positions - rest_start, 0)
    rank_list = jnp.where(in_full, positions // CAP, full_count + rest_pos % others)
    slot_part = jnp.where(in_full, positions % CAP, rest_pos // others)
    tables = []
    counts = []
    for group_number in range(N_DP):
        group_key = jax.random.fold_in(key, 100 + group_number)
        shuffle_key, order_key = jax.random.split(group_key)
        devices = jax.random.permutation(shuffle_key, N_FSDP).astype(jnp.int32)[rank_list]
        entries = devices * CAP + slot_part
        block_order = jax.random.permutation(order_key, group_blocks)
        tables.append(entries[block_order])
        device_ids = jnp.arange(N_FSDP, dtype=jnp.int32)
        counts.append(jnp.sum((devices[:, None] == device_ids[None, :]).astype(jnp.int32), axis=0))
    return (jnp.concatenate(tables).astype(jnp.int32), jnp.stack(counts).astype(jnp.int32))


def draw_owner_table(key, part):
    return owner_layout(key)[0]


def draw_block_counts(key, part):
    return owner_layout(key)[1]


def dominant_stack(key, lower_end, upper_end, spread):
    noise_key, diagonal_key = jax.random.split(key)
    noise = jax.random.normal(noise_key, (SLOTS, B, B), jnp.float32) * (spread / math.sqrt(2.0 * B))
    symmetric = noise + jnp.swapaxes(noise, 1, 2)
    diagonal_part = jnp.exp(jax.random.uniform(diagonal_key, (SLOTS, B), jnp.float32, math.log(lower_end), math.log(upper_end)))
    identity = (jnp.arange(B)[:, None] == jnp.arange(B)[None, :]).astype(jnp.float32)
    return symmetric + identity[None] * diagonal_part[:, :, None]


def draw_stats_left(key, part):
    key = jax.random.fold_in(key, 11)
    matrix = dominant_stack(key, 0.5, 3.0, 0.6)
    return matrix


def draw_stats_right(key, part):
    key = jax.random.fold_in(key, 12)
    matrix = dominant_stack(key, 0.5, 3.0, 0.6)
    return matrix


def draw_precond_left(key, part):
    key = jax.random.fold_in(key, 13)
    matrix = dominant_stack(key, 0.3, 2.0, 0.5)
    return matrix.astype(jnp.bfloat16)


def draw_precond_right(key, part):
    key = jax.random.fold_in(key, 14)
    matrix = dominant_stack(key, 0.3, 2.0, 0.5)
    return matrix.astype(jnp.bfloat16)


def block_levels(own_key, dims, shards, smallest, top_value):
    loudness, own = 1.0, jax.random.fold_in(own_key, 6)
    for axis_at, blocks in shards:
        steps = jnp.exp(jax.random.uniform(jax.random.fold_in(own, axis_at), (blocks,), jnp.float32, smallest / len(shards), top_value / len(shards)))
        loudness = loudness * jnp.repeat(steps, dims[axis_at] // blocks).reshape([-1 if axis == axis_at else 1 for axis in range(len(dims))])
    return loudness


def bell_draw(stream_key, shape, width, most, shards=(), held_as=jnp.bfloat16):
    array = width * jax.random.normal(stream_key, shape, jnp.float32)
    if shards:
        array = array * block_levels(stream_key, shape, shards, -0.22, 0.18)
    return jnp.clip(array, -most, most).astype(held_as)


def setup_inputs(seed: int = 0) -> dict:
    seeds = jax.random.split(jax.random.key(seed), 8)
    return {
        "grads": bell_draw(seeds[0], (N_DP, NBLK, B, B), 0.08, 1.25, ((0, 4), (2, 64))),
        "stats_left": draw_stats_left(jax.random.fold_in(seeds[7], 71), 0),
        "stats_right": draw_stats_right(jax.random.fold_in(seeds[7], 71), 0),
        "precond_left": draw_precond_left(jax.random.fold_in(seeds[7], 71), 0),
        "precond_right": draw_precond_right(jax.random.fold_in(seeds[7], 71), 0),
        "owner_table": draw_owner_table(jax.random.fold_in(seeds[7], 71), 0),
        "block_counts": draw_block_counts(jax.random.fold_in(seeds[7], 71), 0),
    }


BETA = 0.9
EPS = 1e-06

def reference(grads, stats_left, stats_right, precond_left, precond_right, owner_table, block_counts):
    summed = lax.optimization_barrier(jnp.sum(grads.astype(jnp.float32), axis=0))
    mean_grad = (summed * (1.0 / N_DP)).astype(jnp.bfloat16)
    block_ids = jnp.arange(NBLK, dtype=jnp.int32)
    slot_of = block_ids // GBLK * (N_FSDP * CAP) + owner_table.astype(jnp.int32)
    live_all = (jnp.arange(CAP, dtype=jnp.int32)[None, :] < block_counts.reshape(-1)[:, None]).reshape(-1)

    def per_block(block_index):
        block_grad = mean_grad[block_index]
        slot = slot_of[block_index]
        gram_left = jnp.dot(block_grad, block_grad.T, preferred_element_type=jnp.float32)
        gram_right = jnp.dot(block_grad.T, block_grad, preferred_element_type=jnp.float32)
        left_new = BETA * stats_left[slot] + (1.0 - BETA) * gram_left
        right_new = BETA * stats_right[slot] + (1.0 - BETA) * gram_right
        left_part = jnp.dot(precond_left[slot], block_grad, preferred_element_type=jnp.float32).astype(jnp.bfloat16)
        direction = jnp.dot(left_part, precond_right[slot], preferred_element_type=jnp.float32)
        power = jnp.mean(direction * direction)
        scaled = (direction * lax.rsqrt(power + EPS)).astype(jnp.bfloat16)
        return (left_new, right_new, scaled)
    lefts, rights, update = lax.map(per_block, block_ids)
    keep = live_all[slot_of][:, None, None]
    new_left = stats_left.at[slot_of].set(jnp.where(keep, lefts, stats_left[slot_of]))
    new_right = stats_right.at[slot_of].set(jnp.where(keep, rights, stats_right[slot_of]))
    return (new_left, new_right, update)
```

```python
import jax
import jax.numpy as jnp
from jax import lax
from jax.experimental import pallas as pl
from jax.experimental.pallas import tpu as pltpu
from jax.sharding import PartitionSpec as P

BETA = 0.9
EPS = 1e-06
BF16 = jnp.bfloat16
F32 = jnp.float32
SECOND = 8
LIST = 16

VMEM = pl.BlockSpec(memory_space=pltpu.VMEM)
SMEM = pl.BlockSpec(memory_space=pltpu.SMEM)
PARAMS = pltpu.CompilerParams(vmem_limit_bytes=32 * 1024 * 1024)


def shape(*dims, dtype=BF16):
    return jax.ShapeDtypeStruct(dims, dtype)


def call(kernel, outs, scalars, arrays, name, out_specs=None):
    return pl.pallas_call(
        kernel,
        out_shape=outs,
        in_specs=[SMEM] * len(scalars) + [VMEM] * len(arrays),
        out_specs=[VMEM] * len(outs) if out_specs is None else out_specs,
        compiler_params=PARAMS,
        name=name,
    )(*scalars, *arrays)


def split_lists(table, place, grads, replicas, group):
    rows, width = grads.shape[1:]

    def kernel(table_ref, place_ref, grads_ref, first_ref, second_ref, *outs):
        for g in range(replicas):
            in_first = jnp.int32(0)
            in_second = jnp.int32(0)
            for b in range(group):
                odd = table_ref[g * group + b] & 1
                first_ref[g * group + in_first] = b
                second_ref[g * LIST + in_second] = b
                in_first = in_first + (1 - odd)
                in_second = in_second + odd
        for k in range(replicas):
            g = lax.rem(place_ref[0] + k, replicas)
            for i in range(SECOND):
                outs[k][i] = grads_ref[g * group + second_ref[g * LIST + i]]

    outs = [shape(replicas * group, dtype=jnp.int32), shape(replicas * LIST, dtype=jnp.int32)]
    outs += [shape(SECOND, rows, width)] * replicas
    return call(
        kernel, outs, [table, place], [grads], "split", [SMEM, SMEM] + [VMEM] * replicas
    )


def sort_first(first, place, grads, replicas, group):
    rows, width = grads.shape[1:]
    count = group - SECOND

    def kernel(first_ref, place_ref, grads_ref, *outs):
        for k in range(replicas):
            g = lax.rem(place_ref[0] + k, replicas)

            def step(j, _, k=k, g=g):
                outs[k][j] = grads_ref[g * group + first_ref[g * group + j]]
                return 0

            lax.fori_loop(0, count, step, 0, unroll=8)

    return call(
        kernel, [shape(count, rows, width)] * replicas, [first, place], [grads], "sort_first"
    )


def place_mean(table, blocks, stride, count, place, terms, devices, group, name):
    rows, width = terms[0].shape[1:]
    scale = 1.0 / len(terms)

    def kernel(table_ref, blocks_ref, place_ref, *refs):
        out = refs[-1]
        out[...] = jnp.zeros(out.shape, BF16)
        g = place_ref[0]

        def step(j, _):
            owner = table_ref[g * group + blocks_ref[g * stride + j]] >> 1
            total = refs[0][j].astype(F32)
            for term in refs[1:-1]:
                total = total + term[j].astype(F32)
            out[owner] = (total * scale).astype(BF16)
            return 0

        lax.fori_loop(0, count, step, 0, unroll=8)

    return call(kernel, [shape(devices, rows, width)], [table, blocks, place], terms, name)[0]


def precondition(grad, left, right, slot, name):
    size = grad.shape[0]

    def kernel(grad_ref, left_ref, right_ref, out_ref):
        part = jnp.dot(left_ref[0], grad_ref[...], preferred_element_type=F32).astype(BF16)
        direction = jnp.dot(part, right_ref[0], preferred_element_type=F32)
        power = jnp.sum(direction * direction) * (1.0 / (size * size))
        out_ref[...] = (direction * lax.rsqrt(power + EPS)).astype(BF16)

    whole = pl.BlockSpec((size, size), lambda i: (0, 0))
    one = pl.BlockSpec((1, size, size), lambda i: (slot, 0, 0))
    return pl.pallas_call(
        kernel,
        out_shape=shape(size, size),
        grid=(1,),
        in_specs=[whole, one, one],
        out_specs=whole,
        compiler_params=PARAMS,
        name=name,
    )(grad, left, right)


def pick_rows(table, blocks, stride, count, place, pieces, group, name):
    rows, width = pieces.shape[1:]

    def kernel(table_ref, blocks_ref, place_ref, pieces_ref, out):
        g = place_ref[0]

        def step(j, _):
            out[j] = pieces_ref[table_ref[g * group + blocks_ref[g * stride + j]] >> 1]
            return 0

        lax.fori_loop(0, count, step, 0, unroll=8)

    return call(kernel, [shape(count, rows, width)], [table, blocks, place], [pieces], name)[0]


def assemble(first, second, place, firsts, seconds, group):
    replicas = len(firsts)
    rows, width = firsts[0].shape[1:]
    count = group - SECOND

    def kernel(place_ref, first_ref, second_ref, *refs):
        out = refs[-1]
        for k in range(replicas):

            @pl.when(pl.program_id(0) == k)
            def _(k=k):
                g = lax.rem(place_ref[0] + (replicas - k), replicas)

                def step(j, _):
                    out[first_ref[g * group + j]] = refs[k][j]
                    return 0

                lax.fori_loop(0, count, step, 0, unroll=8)
                for i in range(SECOND):
                    out[second_ref[g * LIST + i]] = refs[replicas + k][i]

    whole = lambda count: pl.BlockSpec((count, rows, width), lambda i, *_: (0, 0, 0))
    return pl.pallas_call(
        kernel,
        out_shape=shape(replicas * group, rows, width),
        grid_spec=pltpu.PrefetchScalarGridSpec(
            num_scalar_prefetch=3,
            grid=(replicas,),
            in_specs=[whole(count)] * replicas + [whole(SECOND)] * replicas,
            out_specs=pl.BlockSpec(
                (group, rows, width),
                lambda i, place_ref, *_: (lax.rem(place_ref[0] + (replicas - i), replicas), 0, 0),
            ),
        ),
        compiler_params=PARAMS,
        name="assemble",
    )(place, first, second, *firsts, *seconds)


def shifted(arrays, replicas):
    return [arrays[0]] + [
        lax.ppermute(arrays[k], "dp", [(i, (i + k) % replicas) for i in range(replicas)])
        for k in range(1, replicas)
    ]


def new_statistics(counts, grad_first, grad_second, stats_left, stats_right, parts=2):
    size = stats_left.shape[1]
    tile = size // parts

    def kernel(counts_ref, first_ref, second_ref, left_ref, right_ref, new_left_ref, new_right_ref):
        t = pl.program_id(1)
        for slot, grad_ref in enumerate((first_ref, second_ref)):

            @pl.when(pl.program_id(0) == slot)
            def _(slot=slot, grad_ref=grad_ref):
                live = counts_ref[0] > slot
                for p in range(parts):

                    @pl.when(t == p)
                    def _(p=p):
                        grad = grad_ref[...]
                        span = slice(p * tile, (p + 1) * tile)
                        gram_left = lax.dot_general(
                            grad[span], grad, (((1,), (1,)), ((), ())), preferred_element_type=F32
                        )
                        gram_right = lax.dot_general(
                            grad[:, span], grad, (((0,), (0,)), ((), ())), preferred_element_type=F32
                        )
                        old_left, old_right = left_ref[0], right_ref[0]
                        new_left_ref[0] = jnp.where(
                            live, BETA * old_left + (1.0 - BETA) * gram_left, old_left
                        )
                        new_right_ref[0] = jnp.where(
                            live, BETA * old_right + (1.0 - BETA) * gram_right, old_right
                        )

    whole = pl.BlockSpec((size, size), lambda s, t: (0, 0))
    part = pl.BlockSpec((1, tile, size), lambda s, t: (s, t, 0))
    return pl.pallas_call(
        kernel,
        out_shape=[shape(*stats_left.shape, dtype=F32)] * 2,
        grid=(2, parts),
        in_specs=[SMEM, whole, whole, part, part],
        out_specs=[part, part],
        compiler_params=PARAMS,
        cost_estimate=pl.CostEstimate(
            flops=8 * size**3, bytes_accessed=16 * 2 * size * size, transcendentals=0
        ),
        name="statistics",
    )(counts, grad_first, grad_second, stats_left, stats_right)


def local(grads, stats_left, stats_right, precond_left, precond_right, owner_table, block_counts):
    devices = lax.axis_size("fsdp")
    replicas = lax.axis_size("dp")
    blocks, rows, width = grads.shape[1:]
    size = stats_left.shape[1]
    group = blocks // replicas
    count = group - SECOND
    place = lax.axis_index("dp").astype(jnp.int32).reshape(1)
    mine = grads[0]

    first, second, *second_terms = split_lists(owner_table, place, mine, replicas, group)
    second_terms = shifted(second_terms, replicas)
    first_terms = shifted(sort_first(first, place, mine, replicas, group), replicas)
    second_out = place_mean(
        owner_table, second, LIST, SECOND, place, second_terms, devices, group, "mean_second"
    )
    second_in = lax.all_to_all(second_out, "fsdp", 0, 0, tiled=True)
    first_out = place_mean(
        owner_table, first, group, count, place, first_terms, devices, group, "mean_first"
    )
    first_in = lax.all_to_all(first_out, "fsdp", 0, 0, tiled=True)

    grad_first = first_in.reshape(size, size)
    grad_second = second_in.reshape(size, size)
    scaled_second = precondition(grad_second, precond_left, precond_right, 1, "direction_second")
    scaled_first = precondition(grad_first, precond_left, precond_right, 0, "direction_first")

    first_back = lax.all_to_all(
        scaled_first.reshape(devices, rows, width), "fsdp", 0, 0, tiled=True
    )
    first_rows = pick_rows(
        owner_table, first, group, count, place, first_back, group, "pick_first"
    )
    first_all = shifted([first_rows] * replicas, replicas)
    scaled_second, first_rows = lax.optimization_barrier((scaled_second, first_rows))
    second_back = lax.all_to_all(
        scaled_second.reshape(devices, rows, width), "fsdp", 0, 0, tiled=True
    )
    second_rows = pick_rows(
        owner_table, second, LIST, SECOND, place, second_back, group, "pick_second"
    )
    second_all = shifted([second_rows] * replicas, replicas)
    update = assemble(first, second, place, first_all, second_all, group)

    new_left, new_right = new_statistics(
        block_counts.reshape(1), grad_first, grad_second, stats_left, stats_right
    )
    return (new_left, new_right, update)


def solution(mesh):
    in_specs = (
        P("dp", None, "fsdp", None),
        P(("dp", "fsdp"), None, None),
        P(("dp", "fsdp"), None, None),
        P(("dp", "fsdp"), None, None),
        P(("dp", "fsdp"), None, None),
        P(),
        P("dp", "fsdp"),
    )
    out_specs = (
        P(("dp", "fsdp"), None, None),
        P(("dp", "fsdp"), None, None),
        P(None, "fsdp", None),
    )
    return jax.shard_map(local, mesh=mesh, in_specs=in_specs, out_specs=out_specs, check_vma=False)
```

```python
import jax
import jax.numpy as jnp
from jax import lax
from jax.experimental import pallas as pl
from jax.experimental.pallas import tpu as pltpu
from jax.sharding import PartitionSpec as P

BETA = 0.9
EPS = 1e-06
BF16 = jnp.bfloat16
F32 = jnp.float32

NEXT = [(i, i ^ 1) for i in range(4)]
LAST = [(i, 3 - i) for i in range(4)]

VMEM = pl.BlockSpec(memory_space=pltpu.VMEM)
SMEM = pl.BlockSpec(memory_space=pltpu.SMEM)
HBM = pl.BlockSpec(memory_space=pltpu.HBM)
PARAMS = pltpu.CompilerParams(vmem_limit_bytes=32 * 1024 * 1024)


def shape(*dims, dtype=BF16):
    return jax.ShapeDtypeStruct(dims, dtype)


def call(kernel, outs, in_specs, args, name, scratch=(), out_specs=None):
    return pl.pallas_call(
        kernel,
        out_shape=outs,
        in_specs=in_specs,
        out_specs=[VMEM] * len(outs) if out_specs is None else out_specs,
        scratch_shapes=scratch,
        compiler_params=PARAMS,
        name=name,
    )(*args)


def around():
    me = lax.axis_index("dp")
    return me, me ^ 1, 3 - me, me ^ 2


def first_sends(grads, group):
    rows, width = grads.shape[1:]
    half = width // 2

    def kernel(grads_ref, to_next, to_last, sems):
        _, after, before, opposite = around()
        copies = []
        for out, column, near in ((to_next, 0, after), (to_last, half, before)):
            for at, g in enumerate((near, opposite)):
                source = grads_ref.at[pl.ds(g * group, group), :, pl.ds(column, half)]
                target = out.at[pl.ds(at * group, group)]
                copies.append(pltpu.make_async_copy(source, target, sems.at[len(copies)]))
        for copy in copies:
            copy.start()
        for copy in copies:
            copy.wait()

    outs = [shape(2 * group, rows, half)] * 2
    return call(kernel, outs, [HBM], [grads], "sends", [pltpu.SemaphoreType.DMA((4,))])


def partial_sums(grads, from_next, from_last, group):
    rows, width = grads.shape[1:]
    half = width // 2

    def kernel(grads_ref, from_next_ref, from_last_ref, left, right):
        _, after, before, _ = around()

        def step(j, _):
            kept = grads_ref[before * group + j][:, :half].astype(F32)
            left[j] = (kept + from_next_ref[group + j].astype(F32)).astype(BF16)
            kept = grads_ref[after * group + j][:, half:].astype(F32)
            right[j] = (kept + from_last_ref[group + j].astype(F32)).astype(BF16)
            return 0

        lax.fori_loop(0, group, step, 0, unroll=8)

    outs = [shape(group, rows, half)] * 2
    return call(kernel, outs, [VMEM] * 3, [grads, from_next, from_last], "partial")


def place_mean(table, grads, step_one, step_two, devices, slots, group, replicas):
    rows, width = grads.shape[1:]
    half = width // 2
    scale = 1.0 / replicas

    def kernel(table_ref, grads_ref, *refs):
        out = refs[-1]
        out[...] = jnp.zeros(out.shape, BF16)
        me = lax.axis_index("dp")

        def step(j, _):
            entry = table_ref[me * group + j]
            owner = entry // slots
            column = (entry - owner * slots) * width
            own = grads_ref[me * group + j].astype(F32)
            for c in range(2):
                total = own[:, c * half : (c + 1) * half]
                total = total + refs[c][j].astype(F32) + refs[2 + c][j].astype(F32)
                span = pl.ds(pl.multiple_of(column + c * half, half), half)
                out[owner, :, span] = (total * scale).astype(BF16)
            return 0

        lax.fori_loop(0, group, step, 0, unroll=8)

    outs = [shape(devices, rows, slots * width)]
    args = [table, grads, *step_one, *step_two]
    return call(kernel, outs, [SMEM] + [VMEM] * 5, args, "mean")[0]


def precondition(grads, left, right):
    slots, size = left.shape[:2]

    def kernel(grads_ref, left_ref, right_ref, out_ref):
        for s in range(slots):
            span = slice(s * size, (s + 1) * size)
            part = jnp.dot(
                left_ref[s], grads_ref[:, span], preferred_element_type=F32
            ).astype(BF16)
            direction = jnp.dot(part, right_ref[s], preferred_element_type=F32)
            power = jnp.sum(direction * direction) * (1.0 / (size * size))
            out_ref[:, span] = (direction * lax.rsqrt(power + EPS)).astype(BF16)

    outs = [shape(size, slots * size)]
    return call(kernel, outs, [VMEM] * 3, [grads, left, right], "direction")[0]


def pick_rows(table, pieces, slots, group):
    rows, width = pieces.shape[1], pieces.shape[2] // slots

    def kernel(table_ref, pieces_ref, out):
        me = lax.axis_index("dp")

        def step(j, _):
            entry = table_ref[me * group + j]
            owner = entry // slots
            column = pl.multiple_of((entry - owner * slots) * width, width)
            out[j] = pieces_ref[owner, :, pl.ds(column, width)]
            return 0

        lax.fori_loop(0, group, step, 0, unroll=8)

    return call(kernel, [shape(group, rows, width)], [SMEM, VMEM], [table, pieces], "pick")[0]


def assemble(mine, at_next, at_last, across, replicas):
    group, rows, width = mine.shape

    def kernel(mine_ref, next_ref, last_ref, low_ref, high_ref, out, sems):
        me, after, before, opposite = around()
        parts = (
            (mine_ref, me * group),
            (next_ref, after * group),
            (last_ref, before * group),
            (low_ref, opposite * group),
            (high_ref, opposite * group + group // 2),
        )
        copies = [
            pltpu.make_async_copy(ref, out.at[pl.ds(start, ref.shape[0])], sems.at[i])
            for i, (ref, start) in enumerate(parts)
        ]
        for copy in copies:
            copy.start()
        for copy in copies:
            copy.wait()

    args = [mine, at_next, at_last, *across]
    outs = [shape(replicas * group, rows, width)]
    scratch = [pltpu.SemaphoreType.DMA((5,))]
    return call(kernel, outs, [VMEM] * 5, args, "assemble", scratch, [HBM])[0]


def new_statistics(counts, grads, stats_left, stats_right, parts=2):
    slots, size = stats_left.shape[:2]
    tile = size // parts

    def kernel(counts_ref, grads_ref, left_ref, right_ref, new_left_ref, new_right_ref):
        live = counts_ref[0] > pl.program_id(0)
        for p in range(parts):

            @pl.when(pl.program_id(1) == p)
            def _(p=p):
                grad = grads_ref[...]
                span = slice(p * tile, (p + 1) * tile)
                gram_left = lax.dot_general(
                    grad[span], grad, (((1,), (1,)), ((), ())), preferred_element_type=F32
                )
                gram_right = lax.dot_general(
                    grad[:, span], grad, (((0,), (0,)), ((), ())), preferred_element_type=F32
                )
                old_left, old_right = left_ref[0], right_ref[0]
                new_left_ref[0] = jnp.where(
                    live, BETA * old_left + (1.0 - BETA) * gram_left, old_left
                )
                new_right_ref[0] = jnp.where(
                    live, BETA * old_right + (1.0 - BETA) * gram_right, old_right
                )

    block = pl.BlockSpec((size, size), lambda s, t: (0, s))
    part = pl.BlockSpec((1, tile, size), lambda s, t: (s, t, 0))
    return pl.pallas_call(
        kernel,
        out_shape=[shape(*stats_left.shape, dtype=F32)] * 2,
        grid=(slots, parts),
        in_specs=[SMEM, block, part, part],
        out_specs=[part, part],
        compiler_params=PARAMS,
        cost_estimate=pl.CostEstimate(
            flops=8 * size**3, bytes_accessed=16 * 2 * size * size, transcendentals=0
        ),
        name="statistics",
    )(counts, grads, stats_left, stats_right)


def local(grads, stats_left, stats_right, precond_left, precond_right, owner_table, block_counts):
    devices = lax.axis_size("fsdp")
    replicas = lax.axis_size("dp")
    blocks, rows, width = grads.shape[1:]
    slots, size = stats_left.shape[:2]
    group = blocks // replicas
    mine = grads[0]
    send = lambda pieces, pairs: lax.ppermute(pieces, "dp", pairs)
    exchange = lambda pieces: lax.all_to_all(pieces, "fsdp", 0, 0, tiled=True)

    to_next, to_last = first_sends(mine, group)
    step_one = [send(to_next, NEXT), send(to_last, LAST)]
    left, right = partial_sums(mine, *step_one, group)
    step_two = [send(left, LAST), send(right, NEXT)]
    outgoing = place_mean(
        owner_table, mine, step_one, step_two, devices, slots, group, replicas
    )
    owned = exchange(outgoing).reshape(size, slots * width)

    scaled = precondition(owned, precond_left, precond_right)
    returned = exchange(scaled.reshape(devices, rows, slots * width))
    picked = pick_rows(owner_table, returned, slots, group)
    at_next, at_last = send(picked, NEXT), send(picked, LAST)
    across = [send(at_last[: group // 2], NEXT), send(at_next[group // 2 :], LAST)]
    update = assemble(picked, at_next, at_last, across, replicas)
    new_left, new_right = new_statistics(
        block_counts.reshape(1), owned, stats_left, stats_right
    )
    return (new_left, new_right, update)


def solution(mesh):
    in_specs = (
        P("dp", None, "fsdp", None),
        P(("dp", "fsdp"), None, None),
        P(("dp", "fsdp"), None, None),
        P(("dp", "fsdp"), None, None),
        P(("dp", "fsdp"), None, None),
        P(),
        P("dp", "fsdp"),
    )
    out_specs = (
        P(("dp", "fsdp"), None, None),
        P(("dp", "fsdp"), None, None),
        P(None, "fsdp", None),
    )
    return jax.shard_map(local, mesh=mesh, in_specs=in_specs, out_specs=out_specs, check_vma=False)
```

```python
import jax
import jax.numpy as jnp
from jax import lax
from jax.experimental import pallas as pl
from jax.experimental.pallas import tpu as pltpu
from jax.sharding import PartitionSpec as P

BETA = 0.9
EPS = 1e-06
BF16 = jnp.bfloat16
F32 = jnp.float32

NEXT = [(i, i ^ 1) for i in range(4)]
LAST = [(i, 3 - i) for i in range(4)]
OPPOSITE = [(i, i ^ 2) for i in range(4)]
SECOND = 8
LIST = 16

VMEM = pl.BlockSpec(memory_space=pltpu.VMEM)
SMEM = pl.BlockSpec(memory_space=pltpu.SMEM)
HBM = pl.BlockSpec(memory_space=pltpu.HBM)
PARAMS = pltpu.CompilerParams(vmem_limit_bytes=16 * 1024 * 1024)


def shape(*dims, dtype=BF16):
    return jax.ShapeDtypeStruct(dims, dtype)


def call(kernel, outs, in_specs, args, name, scratch=(), out_specs=None):
    return pl.pallas_call(
        kernel,
        out_shape=outs,
        in_specs=in_specs,
        out_specs=[VMEM] * len(outs) if out_specs is None else out_specs,
        scratch_shapes=scratch,
        compiler_params=PARAMS,
        name=name,
    )(*args)


def around():
    me = lax.axis_index("dp")
    return me, me ^ 1, 3 - me, me ^ 2


def copy_all(pairs, sems):
    copies = [
        pltpu.make_async_copy(source, target, sems.at[i])
        for i, (source, target) in enumerate(pairs)
    ]
    for copy in copies:
        copy.start()
    for copy in copies:
        copy.wait()


def first_sends(grads, group):
    rows, width = grads.shape[1:]
    half = width // 2

    def kernel(grads_ref, far_next, far_last, near_next, near_last, sems):
        _, after, before, opposite = around()
        part = lambda g, column: grads_ref.at[pl.ds(g * group, group), :, pl.ds(column, half)]
        pairs = [
            (part(opposite, 0), far_next),
            (part(opposite, half), far_last),
            (part(after, 0), near_next),
            (part(before, half), near_last),
        ]
        copy_all(pairs, sems)

    outs = [shape(group, rows, half)] * 4
    scratch = [pltpu.SemaphoreType.DMA((4,))]
    return call(kernel, outs, [HBM], [grads], "sends", scratch)


def kept(grads, group):
    rows, width = grads.shape[1:]
    half = width // 2

    def kernel(grads_ref, own, left, right, sems):
        me, after, before, _ = around()
        part = lambda g, column: grads_ref.at[pl.ds(g * group, group), :, pl.ds(column, half)]
        pairs = [
            (grads_ref.at[pl.ds(me * group, group)], own),
            (part(before, 0), left),
            (part(after, half), right),
        ]
        copy_all(pairs, sems)

    outs = [shape(group, rows, width)] + [shape(group, rows, half)] * 2
    scratch = [pltpu.SemaphoreType.DMA((3,))]
    return call(kernel, outs, [HBM], [grads], "kept", scratch)


def partial_sums(kept_halves, arrived):
    dims = arrived[0].shape

    def kernel(left_kept, right_kept, left_got, right_got, left, right):
        def step(j, _):
            left[j] = (left_kept[j].astype(F32) + left_got[j].astype(F32)).astype(BF16)
            right[j] = (right_kept[j].astype(F32) + right_got[j].astype(F32)).astype(BF16)
            return 0

        lax.fori_loop(0, dims[0], step, 0, unroll=8)

    return call(kernel, [shape(*dims)] * 2, [VMEM] * 4, [*kept_halves, *arrived], "partial")


def place_mean(table, own, near, passed, devices, replicas):
    group, rows, width = own.shape
    half = width // 2
    scale = 1.0 / replicas

    def kernel(table_ref, own_ref, *refs):
        first, second = refs[-2:]
        first[...] = jnp.zeros(first.shape, BF16)
        second[...] = jnp.zeros(second.shape, BF16)
        me = lax.axis_index("dp")

        def step(j, _):
            entry = table_ref[me * group + j]
            own = own_ref[j].astype(F32)
            halves = []
            for c in range(2):
                total = own[:, c * half : (c + 1) * half]
                total = total + refs[c][j].astype(F32) + refs[2 + c][j].astype(F32)
                halves.append((total * scale).astype(BF16))
            for slot, out in enumerate((first, second)):

                @pl.when((entry & 1) == slot)
                def _(out=out):
                    for c in range(2):
                        out[entry >> 1, :, c * half : (c + 1) * half] = halves[c]

            return 0

        lax.fori_loop(0, group, step, 0, unroll=8)

    outs = [shape(devices, rows, width)] * 2
    args = [table, own, *near, *passed]
    return call(kernel, outs, [SMEM] + [VMEM] * 5, args, "mean")


def scaled_update(grad, left, right):
    part = jnp.dot(left, grad, preferred_element_type=F32).astype(BF16)
    direction = jnp.dot(part, right, preferred_element_type=F32)
    power = jnp.sum(direction * direction) * (1.0 / (direction.shape[0] * direction.shape[1]))
    return (direction * lax.rsqrt(power + EPS)).astype(BF16)


def direction_first(grad, left, right, passenger):
    size = grad.shape[0]

    def kernel(grad_ref, left_ref, right_ref, passenger_ref, out):
        out[:, size:] = passenger_ref[...]
        out[:, :size] = scaled_update(grad_ref[...], left_ref[0], right_ref[0])

    whole = pl.BlockSpec((size, size), lambda i: (0, 0))
    slot = pl.BlockSpec((1, size, size), lambda i: (0, 0, 0))
    return pl.pallas_call(
        kernel,
        out_shape=shape(size, 2 * size),
        grid=(1,),
        in_specs=[whole, slot, slot, whole],
        out_specs=pl.BlockSpec((size, 2 * size), lambda i: (0, 0)),
        compiler_params=PARAMS,
        name="direction_first",
    )(grad, left, right, passenger)


def direction_second(mixed, left, right):
    size = mixed.shape[0]

    def kernel(grad_ref, left_ref, right_ref, out):
        out[...] = scaled_update(grad_ref[...], left_ref[0], right_ref[0])

    slot = pl.BlockSpec((1, size, size), lambda i: (1, 0, 0))
    return pl.pallas_call(
        kernel,
        out_shape=shape(size, size),
        grid=(1,),
        in_specs=[pl.BlockSpec((size, size), lambda i: (0, 1)), slot, slot],
        out_specs=pl.BlockSpec((size, size), lambda i: (0, 0)),
        compiler_params=PARAMS,
        name="direction_second",
    )(mixed, left, right)


def pick_first(table, pieces, group):
    rows, width = pieces.shape[1], pieces.shape[2] // 2
    half = group // 2

    def kernel(table_ref, pieces_ref, low, high):
        me = lax.axis_index("dp")

        def step(j, _):
            low[j] = pieces_ref[table_ref[me * group + j] >> 1]
            high[j] = pieces_ref[table_ref[me * group + half + j] >> 1]
            return 0

        lax.fori_loop(0, half, step, 0, unroll=8)

    return pl.pallas_call(
        kernel,
        out_shape=[shape(half, rows, width)] * 2,
        grid=(1,),
        in_specs=[SMEM, pl.BlockSpec((pieces.shape[0], rows, width), lambda i: (0, 0, 0))],
        out_specs=[pl.BlockSpec((half, rows, width), lambda i: (0, 0, 0))] * 2,
        compiler_params=PARAMS,
        name="pick_first",
    )(table, pieces)


def pick_second(table, pieces, group):
    rows, width = pieces.shape[1:]

    def kernel(table_ref, pieces_ref, out, room):
        me = lax.axis_index("dp")
        count = jnp.int32(0)
        for j in range(group):
            entry = table_ref[me * group + j]
            room[count] = pieces_ref[entry >> 1]
            count = count + (entry & 1)
        for i in range(SECOND):
            out[i] = room[i]

    outs = [shape(SECOND, rows, width)]
    scratch = [pltpu.VMEM((SECOND + 1, rows, width), BF16)]
    return call(kernel, outs, [SMEM, VMEM], [table, pieces], "pick_second", scratch)[0]


def second_places(table, group, replicas):
    def kernel(table_ref, at):
        for g in range(replicas):
            count = jnp.int32(0)
            for j in range(group):
                at[g * LIST + count] = g * group + j
                count = count + (table_ref[g * group + j] & 1)

    outs = [shape(replicas * LIST, dtype=jnp.int32)]
    return call(kernel, outs, [SMEM], [table], "second_places", out_specs=[SMEM])[0]


def lay_near(near, group, replicas):
    rows, width = near[0].shape[1:]

    def kernel(*refs):
        sources, (out, sems) = refs[:-2], refs[-2:]
        starts = [g * group + i * (group // 2) for g in around()[:3] for i in range(2)]
        pairs = [
            (source, out.at[pl.ds(start, group // 2)])
            for source, start in zip(sources, starts)
        ]
        copy_all(pairs, sems)

    outs = [shape(replicas * group, rows, width)]
    scratch = [pltpu.SemaphoreType.DMA((len(near),))]
    return call(kernel, outs, [VMEM] * len(near), near, "lay_near", scratch, [HBM])[0]


def lay_rest(update, at, across, seconds, group):
    replicas = len(seconds)

    def kernel(at_ref, _, low, high, *refs):
        sources, (out, sems, second_sems) = refs[:replicas], refs[replicas:]
        groups = around()
        start = groups[-1] * group
        copies = [
            pltpu.make_async_copy(ref, out.at[pl.ds(start + i * (group // 2), group // 2)], sems.at[i])
            for i, ref in enumerate((low, high))
        ]
        for copy in copies:
            copy.start()
        for k, g in enumerate(groups):
            if k == replicas - 1:
                for copy in copies:
                    copy.wait()
            for i in range(SECOND):
                pltpu.make_async_copy(
                    sources[k].at[i], out.at[at_ref[g * LIST + i]], second_sems.at[k]
                ).start()
        for k in range(replicas):
            pltpu.make_async_copy(
                sources[k], out.at[pl.ds(0, SECOND)], second_sems.at[k]
            ).wait()

    return pl.pallas_call(
        kernel,
        out_shape=shape(*update.shape),
        in_specs=[SMEM, HBM] + [VMEM] * (2 + replicas),
        out_specs=HBM,
        scratch_shapes=[pltpu.SemaphoreType.DMA((2,)), pltpu.SemaphoreType.DMA((replicas,))],
        input_output_aliases={1: 0},
        compiler_params=PARAMS,
        name="lay_rest",
    )(at, update, *across, *seconds)


def new_statistics(counts, grad, mixed, stats_left, stats_right, parts=2):
    slots, size = stats_left.shape[:2]
    tile = size // parts

    def kernel(counts_ref, first, second, left_ref, right_ref, new_left_ref, new_right_ref):
        live = counts_ref[0] > pl.program_id(0)
        for s, p in [(s, p) for s in range(slots) for p in range(parts)]:

            @pl.when((pl.program_id(0) == s) & (pl.program_id(1) == p))
            def _(s=s, p=p):
                grad = (first, second)[s][...]
                span = slice(p * tile, (p + 1) * tile)
                gram_left = lax.dot_general(
                    grad[span], grad, (((1,), (1,)), ((), ())), preferred_element_type=F32
                )
                gram_right = lax.dot_general(
                    grad[:, span], grad, (((0,), (0,)), ((), ())), preferred_element_type=F32
                )
                old_left, old_right = left_ref[0], right_ref[0]
                new_left_ref[0] = jnp.where(
                    live, BETA * old_left + (1.0 - BETA) * gram_left, old_left
                )
                new_right_ref[0] = jnp.where(
                    live, BETA * old_right + (1.0 - BETA) * gram_right, old_right
                )

    block = lambda column: pl.BlockSpec((size, size), lambda s, t: (0, column))
    part = pl.BlockSpec((1, tile, size), lambda s, t: (s, t, 0))
    return pl.pallas_call(
        kernel,
        out_shape=[shape(*stats_left.shape, dtype=F32)] * 2,
        grid=(slots, parts),
        in_specs=[SMEM, block(0), block(1), part, part],
        out_specs=[part, part],
        compiler_params=PARAMS,
        cost_estimate=pl.CostEstimate(
            flops=8 * size**3, bytes_accessed=16 * 2 * size * size, transcendentals=0
        ),
        name="statistics",
    )(counts, grad, mixed, stats_left, stats_right)


def local(grads, stats_left, stats_right, precond_left, precond_right, owner_table, block_counts):
    devices = lax.axis_size("fsdp")
    replicas = lax.axis_size("dp")
    blocks, rows, width = grads.shape[1:]
    slots, size = stats_left.shape[:2]
    group = blocks // replicas
    mine = grads[0]
    send = lambda pieces, pairs: lax.ppermute(pieces, "dp", pairs)
    exchange = lambda pieces: lax.all_to_all(pieces, "fsdp", 0, 0, tiled=True)

    far_next, far_last, near_next, near_last = first_sends(mine, group)
    own, *kept_halves = kept(mine, group)
    arrived = [send(far_next, NEXT), send(far_last, LAST)]
    near = [send(near_next, NEXT), send(near_last, LAST)]
    at = second_places(owner_table, group, replicas)
    kept_halves, at = lax.optimization_barrier((kept_halves, at))
    left, right = partial_sums(kept_halves, arrived)
    passed = [send(left, LAST), send(right, NEXT)]
    first_out, second_out = place_mean(owner_table, own, near, passed, devices, replicas)
    grad_first = exchange(first_out).reshape(size, width)
    outgoing = direction_first(
        grad_first, precond_left, precond_right, second_out.reshape(size, width)
    )
    mixed = exchange(outgoing.reshape(devices, rows, 2 * width))
    mixed_rows = mixed.reshape(size, 2 * width)
    scaled_second = direction_second(mixed_rows, precond_left, precond_right)
    second_back = exchange(scaled_second.reshape(devices, rows, width))

    low, high = pick_first(owner_table, mixed, group)
    last_low, next_high = send(low, LAST), send(high, NEXT)
    next_low, last_high = send(low, NEXT), send(high, LAST)
    grad_first, _ = lax.optimization_barrier((grad_first, low))
    stats = new_statistics(
        block_counts.reshape(1), grad_first, mixed_rows, stats_left, stats_right
    )
    last_low, next_high, stats = lax.optimization_barrier((last_low, next_high, stats))
    across = [send(last_low, NEXT), send(next_high, LAST)]
    second_rows = pick_second(owner_table, second_back, group)
    seconds = [second_rows] + [send(second_rows, p) for p in (NEXT, LAST, OPPOSITE)]
    update = lay_near([low, high, next_low, next_high, last_low, last_high], group, replicas)
    update = lay_rest(update, at, across, seconds, group)
    return (*stats, update)


def solution(mesh):
    in_specs = (
        P("dp", None, "fsdp", None),
        P(("dp", "fsdp"), None, None),
        P(("dp", "fsdp"), None, None),
        P(("dp", "fsdp"), None, None),
        P(("dp", "fsdp"), None, None),
        P(),
        P("dp", "fsdp"),
    )
    out_specs = (
        P(("dp", "fsdp"), None, None),
        P(("dp", "fsdp"), None, None),
        P(None, "fsdp", None),
    )
    return jax.shard_map(local, mesh=mesh, in_specs=in_specs, out_specs=out_specs, check_vma=False)
```

```python
import jax
import jax.numpy as jnp
from jax import lax
from jax.experimental import pallas as pl
from jax.experimental.pallas import tpu as pltpu
from jax.sharding import PartitionSpec as P

BETA = 0.9
EPS = 1e-06
BF16 = jnp.bfloat16
F32 = jnp.float32

NEXT = [(i, i ^ 1) for i in range(4)]
LAST = [(i, 3 - i) for i in range(4)]
OPPOSITE = [(i, i ^ 2) for i in range(4)]
SECOND = 8
LIST = 16

VMEM = pl.BlockSpec(memory_space=pltpu.VMEM)
SMEM = pl.BlockSpec(memory_space=pltpu.SMEM)
HBM = pl.BlockSpec(memory_space=pltpu.HBM)
PARAMS = pltpu.CompilerParams(vmem_limit_bytes=16 * 1024 * 1024)


def shape(*dims, dtype=BF16):
    return jax.ShapeDtypeStruct(dims, dtype)


def call(kernel, outs, in_specs, args, name, scratch=(), out_specs=None):
    return pl.pallas_call(
        kernel,
        out_shape=outs,
        in_specs=in_specs,
        out_specs=[VMEM] * len(outs) if out_specs is None else out_specs,
        scratch_shapes=scratch,
        compiler_params=PARAMS,
        name=name,
    )(*args)


def around():
    me = lax.axis_index("dp")
    return me, me ^ 1, 3 - me, me ^ 2


def copy_all(pairs, sems):
    copies = [
        pltpu.make_async_copy(source, target, sems.at[i])
        for i, (source, target) in enumerate(pairs)
    ]
    for copy in copies:
        copy.start()
    for copy in copies:
        copy.wait()


def first_sends(grads, group):
    rows, width = grads.shape[1:]
    half = group // 2

    def kernel(grads_ref, far_next, far_last, near_next, near_last, sems):
        _, after, before, opposite = around()
        part = lambda g, i: grads_ref.at[pl.ds(g * group + i * half, half)]
        pairs = [
            (part(opposite, 0), far_next),
            (part(opposite, 1), far_last),
            (part(after, 0), near_next),
            (part(before, 1), near_last),
        ]
        copy_all(pairs, sems)

    outs = [shape(half, rows, width)] * 4
    return call(kernel, outs, [HBM], [grads], "sends", [pltpu.SemaphoreType.DMA((4,))])


def kept(grads, group):
    rows, width = grads.shape[1:]
    half = group // 2

    def kernel(grads_ref, own, low, high, sems):
        me, after, before, _ = around()
        part = lambda g, i, count: grads_ref.at[pl.ds(g * group + i * half, count)]
        pairs = [(part(me, 0, group), own), (part(before, 0, half), low), (part(after, 1, half), high)]
        copy_all(pairs, sems)

    outs = [shape(group, rows, width)] + [shape(half, rows, width)] * 2
    return call(kernel, outs, [HBM], [grads], "kept", [pltpu.SemaphoreType.DMA((3,))])


def partial_sums(kept_halves, arrived):
    dims = arrived[0].shape

    def kernel(low_kept, high_kept, low_got, high_got, low, high):
        def step(j, _):
            low[j] = (low_kept[j].astype(F32) + low_got[j].astype(F32)).astype(BF16)
            high[j] = (high_kept[j].astype(F32) + high_got[j].astype(F32)).astype(BF16)
            return 0

        lax.fori_loop(0, dims[0], step, 0, unroll=8)

    return call(kernel, [shape(*dims)] * 2, [VMEM] * 4, [*kept_halves, *arrived], "partial")


def place_mean(table, own, near, passed, devices, replicas):
    group, rows, width = own.shape
    half = group // 2
    scale = 1.0 / replicas

    def kernel(table_ref, own_ref, *refs):
        halves, (first, second, room) = refs[:4], refs[4:]
        room[...] = jnp.zeros(room.shape, BF16)
        me = lax.axis_index("dp")

        def step(j, _):
            for i in range(2):
                entry = table_ref[me * group + i * half + j]
                total = own_ref[i * half + j].astype(F32) + halves[i][j].astype(F32)
                total = total + halves[2 + i][j].astype(F32)
                room[(entry & 1) * devices + (entry >> 1)] = (total * scale).astype(BF16)
            return 0

        lax.fori_loop(0, half, step, 0, unroll=8)
        first[...] = room[:devices]
        second[...] = room[devices:]

    outs = [shape(devices, rows, width)] * 2
    args = [table, own, *near, *passed]
    scratch = [pltpu.VMEM((2 * devices, rows, width), BF16)]
    return call(kernel, outs, [SMEM] + [VMEM] * 5, args, "mean", scratch)


def direction_and_scale(grad, left, right):
    part = jnp.dot(left, grad, preferred_element_type=F32).astype(BF16)
    direction = jnp.dot(part, right, preferred_element_type=F32)
    power = jnp.sum(direction * direction) * (1.0 / (direction.shape[0] * direction.shape[1]))
    return direction, lax.rsqrt(power + EPS)


def direction_first(grad, left, right, passenger):
    size = grad.shape[0]

    def kernel(grad_ref, left_ref, right_ref, passenger_ref, out):
        out[:, size:] = passenger_ref[...]
        direction, scale = direction_and_scale(grad_ref[...], left_ref[0], right_ref[0])
        out[:, :size] = (direction * scale).astype(BF16)

    whole = pl.BlockSpec((size, size), lambda i: (0, 0))
    slot = pl.BlockSpec((1, size, size), lambda i: (0, 0, 0))
    return pl.pallas_call(
        kernel,
        out_shape=shape(size, 2 * size),
        grid=(1,),
        in_specs=[whole, slot, slot, whole],
        out_specs=pl.BlockSpec((size, 2 * size), lambda i: (0, 0)),
        compiler_params=PARAMS,
        name="direction_first",
    )(grad, left, right, passenger)


def direction_second(mixed, left, right, parts=2):
    size = mixed.shape[0]
    tile = size // parts

    def kernel(grad_ref, left_ref, right_ref, out, room, sems):
        direction, scale = direction_and_scale(grad_ref[...], left_ref[0], right_ref[0])
        copies = []
        for p in range(parts):
            span = pl.ds(p * tile, tile)
            room[span] = (direction[p * tile : (p + 1) * tile] * scale).astype(BF16)
            copies.append(pltpu.make_async_copy(room.at[span], out.at[span], sems.at[p]))
            copies[-1].start()
        for copy in copies:
            copy.wait()

    slot = pl.BlockSpec((1, size, size), lambda i: (1, 0, 0))
    return pl.pallas_call(
        kernel,
        out_shape=shape(size, size),
        grid=(1,),
        in_specs=[pl.BlockSpec((size, size), lambda i: (0, 1)), slot, slot],
        out_specs=HBM,
        scratch_shapes=[pltpu.VMEM((size, size), BF16), pltpu.SemaphoreType.DMA((parts,))],
        compiler_params=PARAMS,
        name="direction_second",
    )(mixed, left, right)


def pick_first(table, pieces, group):
    rows, width = pieces.shape[1], pieces.shape[2] // 2
    half = group // 2

    def kernel(table_ref, pieces_ref, low, high):
        me = lax.axis_index("dp")

        def step(j, _):
            low[j] = pieces_ref[table_ref[me * group + j] >> 1]
            high[j] = pieces_ref[table_ref[me * group + half + j] >> 1]
            return 0

        lax.fori_loop(0, half, step, 0, unroll=8)

    return pl.pallas_call(
        kernel,
        out_shape=[shape(half, rows, width)] * 2,
        grid=(1,),
        in_specs=[SMEM, pl.BlockSpec((pieces.shape[0], rows, width), lambda i: (0, 0, 0))],
        out_specs=[pl.BlockSpec((half, rows, width), lambda i: (0, 0, 0))] * 2,
        compiler_params=PARAMS,
        name="pick_first",
    )(table, pieces)


def pick_second(table, at, pieces):
    rows, width = pieces.shape[1:]

    def kernel(table_ref, at_ref, pieces_ref, out, sem):
        me = lax.axis_index("dp")
        for i in range(SECOND):
            owner = table_ref[at_ref[me * LIST + i]] >> 1
            pltpu.make_async_copy(pieces_ref.at[owner], out.at[i], sem).start()
        pltpu.make_async_copy(pieces_ref.at[pl.ds(0, SECOND)], out, sem).wait()

    outs = [shape(SECOND, rows, width)]
    scratch = [pltpu.SemaphoreType.DMA]
    args = [table, at, pieces]
    return call(kernel, outs, [SMEM, SMEM, HBM], args, "pick_second", scratch)[0]


def second_places(table, group, replicas):
    def kernel(table_ref, at):
        for g in range(replicas):
            count = jnp.int32(0)
            for j in range(group):
                at[g * LIST + count] = g * group + j
                count = count + (table_ref[g * group + j] & 1)

    outs = [shape(replicas * LIST, dtype=jnp.int32)]
    return call(kernel, outs, [SMEM], [table], "second_places", out_specs=[SMEM])[0]


def lay_near(near, group, replicas):
    rows, width = near[0].shape[1:]

    def kernel(*refs):
        sources, (out, sems) = refs[:-2], refs[-2:]
        starts = [g * group + i * (group // 2) for g in around()[:3] for i in range(2)]
        pairs = [
            (source, out.at[pl.ds(start, group // 2)])
            for source, start in zip(sources, starts)
        ]
        copy_all(pairs, sems)

    outs = [shape(replicas * group, rows, width)]
    scratch = [pltpu.SemaphoreType.DMA((len(near),))]
    return call(kernel, outs, [VMEM] * len(near), near, "lay_near", scratch, [HBM])[0]


def lay_across(update, across, group):
    def kernel(_, low, high, out, sems):
        start = around()[-1] * group
        pairs = [
            (ref, out.at[pl.ds(start + i * (group // 2), group // 2)])
            for i, ref in enumerate((low, high))
        ]
        copy_all(pairs, sems)

    return pl.pallas_call(
        kernel,
        out_shape=shape(*update.shape),
        in_specs=[HBM, VMEM, VMEM],
        out_specs=HBM,
        scratch_shapes=[pltpu.SemaphoreType.DMA((2,))],
        input_output_aliases={0: 0},
        compiler_params=PARAMS,
        name="lay_across",
    )(update, *across)


def lay_second(update, at, seconds):
    replicas = len(seconds)

    def kernel(at_ref, _, *refs):
        sources, (out, sems) = refs[:replicas], refs[replicas:]
        for k, g in enumerate(around()):
            for i in range(SECOND):
                pltpu.make_async_copy(
                    sources[k].at[i], out.at[at_ref[g * LIST + i]], sems.at[k]
                ).start()
        for k in range(replicas):
            pltpu.make_async_copy(sources[k], out.at[pl.ds(0, SECOND)], sems.at[k]).wait()

    return pl.pallas_call(
        kernel,
        out_shape=shape(*update.shape),
        in_specs=[SMEM, HBM] + [VMEM] * replicas,
        out_specs=HBM,
        scratch_shapes=[pltpu.SemaphoreType.DMA((replicas,))],
        input_output_aliases={1: 0},
        compiler_params=PARAMS,
        name="lay_second",
    )(at, update, *seconds)


def new_statistics(counts, grad, mixed, stats_left, stats_right, parts=2):
    slots, size = stats_left.shape[:2]
    tile = size // parts

    def kernel(counts_ref, first, second, left_ref, right_ref, new_left_ref, new_right_ref):
        live = counts_ref[0] > pl.program_id(0)
        for s, p in [(s, p) for s in range(slots) for p in range(parts)]:

            @pl.when((pl.program_id(0) == s) & (pl.program_id(1) == p))
            def _(s=s, p=p):
                grad = (first, second)[s][...]
                span = slice(p * tile, (p + 1) * tile)
                gram_left = lax.dot_general(
                    grad[span], grad, (((1,), (1,)), ((), ())), preferred_element_type=F32
                )
                gram_right = lax.dot_general(
                    grad[:, span], grad, (((0,), (0,)), ((), ())), preferred_element_type=F32
                )
                old_left, old_right = left_ref[0], right_ref[0]
                new_left_ref[0] = jnp.where(
                    live, BETA * old_left + (1.0 - BETA) * gram_left, old_left
                )
                new_right_ref[0] = jnp.where(
                    live, BETA * old_right + (1.0 - BETA) * gram_right, old_right
                )

    block = lambda column: pl.BlockSpec((size, size), lambda s, t: (0, column))
    part = pl.BlockSpec((1, tile, size), lambda s, t: (s, t, 0))
    return pl.pallas_call(
        kernel,
        out_shape=[shape(*stats_left.shape, dtype=F32)] * 2,
        grid=(slots, parts),
        in_specs=[SMEM, block(0), block(1), part, part],
        out_specs=[part, part],
        compiler_params=PARAMS,
        cost_estimate=pl.CostEstimate(
            flops=8 * size**3, bytes_accessed=16 * 2 * size * size, transcendentals=0
        ),
        name="statistics",
    )(counts, grad, mixed, stats_left, stats_right)


def local(grads, stats_left, stats_right, precond_left, precond_right, owner_table, block_counts):
    devices = lax.axis_size("fsdp")
    replicas = lax.axis_size("dp")
    blocks, rows, width = grads.shape[1:]
    slots, size = stats_left.shape[:2]
    group = blocks // replicas
    mine = pltpu.with_memory_space_constraint(grads[0], pltpu.HBM)
    send = lambda pieces, pairs: lax.ppermute(pieces, "dp", pairs)
    exchange = lambda pieces: lax.all_to_all(pieces, "fsdp", 0, 0, tiled=True)

    far_next, far_last, near_next, near_last = first_sends(mine, group)
    own, *kept_halves = kept(mine, group)
    arrived = [send(far_next, NEXT), send(far_last, LAST)]
    near = [send(near_next, NEXT), send(near_last, LAST)]
    at = second_places(owner_table, group, replicas)
    kept_halves, at = lax.optimization_barrier((kept_halves, at))
    low, high = partial_sums(kept_halves, arrived)
    passed = [send(low, LAST), send(high, NEXT)]
    first_out, second_out = place_mean(owner_table, own, near, passed, devices, replicas)
    grad_first = exchange(first_out).reshape(size, width)
    outgoing = direction_first(
        grad_first, precond_left, precond_right, second_out.reshape(size, width)
    )
    mixed = exchange(outgoing.reshape(devices, rows, 2 * width))
    mixed_rows = mixed.reshape(size, 2 * width)
    scaled_second = direction_second(mixed_rows, precond_left, precond_right)
    second_back = exchange(scaled_second.reshape(devices, rows, width))

    low, high = pick_first(owner_table, mixed, group)
    last_low, next_high = send(low, LAST), send(high, NEXT)
    next_low, last_high = send(low, NEXT), send(high, LAST)
    grad_first, _ = lax.optimization_barrier((grad_first, low))
    stats = new_statistics(
        block_counts.reshape(1), grad_first, mixed_rows, stats_left, stats_right
    )
    last_low, next_high, stats = lax.optimization_barrier((last_low, next_high, stats))
    across = [send(last_low, NEXT), send(next_high, LAST)]
    second_rows = pick_second(owner_table, at, second_back)
    seconds = [second_rows] + [send(second_rows, p) for p in (NEXT, LAST, OPPOSITE)]
    update = lay_near([low, high, next_low, next_high, last_low, last_high], group, replicas)
    update = lay_across(update, across, group)
    update = lay_second(update, at, seconds)
    return (*stats, update)


def solution(mesh):
    in_specs = (
        P("dp", None, "fsdp", None),
        P(("dp", "fsdp"), None, None),
        P(("dp", "fsdp"), None, None),
        P(("dp", "fsdp"), None, None),
        P(("dp", "fsdp"), None, None),
        P(),
        P("dp", "fsdp"),
    )
    out_specs = (
        P(("dp", "fsdp"), None, None),
        P(("dp", "fsdp"), None, None),
        P(None, "fsdp", None),
    )
    return jax.shard_map(local, mesh=mesh, in_specs=in_specs, out_specs=out_specs, check_vma=False)
```

```python
import jax
import jax.numpy as jnp
from jax import lax
from jax.experimental import pallas as pl
from jax.experimental.pallas import tpu as pltpu
from jax.sharding import PartitionSpec as P

BETA = 0.9
EPS = 1e-06
BF16 = jnp.bfloat16
F32 = jnp.float32

NEXT = [(i, i ^ 1) for i in range(4)]
LAST = [(i, 3 - i) for i in range(4)]
OPPOSITE = [(i, i ^ 2) for i in range(4)]
SECOND = 8
LIST = 16

VMEM = pl.BlockSpec(memory_space=pltpu.VMEM)
SMEM = pl.BlockSpec(memory_space=pltpu.SMEM)
HBM = pl.BlockSpec(memory_space=pltpu.HBM)
PARAMS = pltpu.CompilerParams(vmem_limit_bytes=16 * 1024 * 1024)


def shape(*dims, dtype=BF16):
    return jax.ShapeDtypeStruct(dims, dtype)


def call(kernel, outs, in_specs, args, name, scratch=(), out_specs=None):
    return pl.pallas_call(
        kernel,
        out_shape=outs,
        in_specs=in_specs,
        out_specs=[VMEM] * len(outs) if out_specs is None else out_specs,
        scratch_shapes=scratch,
        compiler_params=PARAMS,
        name=name,
    )(*args)


def around():
    me = lax.axis_index("dp")
    return me, me ^ 1, 3 - me, me ^ 2


def copy_all(pairs, sems):
    copies = [
        pltpu.make_async_copy(source, target, sems.at[i])
        for i, (source, target) in enumerate(pairs)
    ]
    for copy in copies:
        copy.start()
    for copy in copies:
        copy.wait()


def first_sends(grads, group, far):
    rows, width = grads.shape[1:]
    half = group // 2

    def kernel(grads_ref, to_next, to_last, sems):
        _, after, before, opposite = around()
        groups = (opposite, opposite) if far else (after, before)
        pairs = [
            (grads_ref.at[pl.ds(g * group + i * half, half)], out)
            for i, (g, out) in enumerate(zip(groups, (to_next, to_last)))
        ]
        copy_all(pairs, sems)

    outs = [shape(half, rows, width)] * 2
    name = "far_sends" if far else "near_sends"
    return call(kernel, outs, [HBM], [grads], name, [pltpu.SemaphoreType.DMA((2,))])


def kept(grads, group):
    rows, width = grads.shape[1:]
    half = group // 2

    def kernel(grads_ref, own, low, high, sems):
        me, after, before, _ = around()
        part = lambda g, i, count: grads_ref.at[pl.ds(g * group + i * half, count)]
        pairs = [(part(me, 0, group), own), (part(before, 0, half), low), (part(after, 1, half), high)]
        copy_all(pairs, sems)

    outs = [shape(group, rows, width)] + [shape(half, rows, width)] * 2
    return call(kernel, outs, [HBM], [grads], "kept", [pltpu.SemaphoreType.DMA((3,))])


def partial_sums(kept_halves, arrived):
    dims = arrived[0].shape

    def kernel(low_kept, high_kept, low_got, high_got, low, high):
        def step(j, _):
            low[j] = (low_kept[j].astype(F32) + low_got[j].astype(F32)).astype(BF16)
            high[j] = (high_kept[j].astype(F32) + high_got[j].astype(F32)).astype(BF16)
            return 0

        lax.fori_loop(0, dims[0], step, 0, unroll=8)

    return call(kernel, [shape(*dims)] * 2, [VMEM] * 4, [*kept_halves, *arrived], "partial")


def place_mean(table, own, near, passed, devices, slots, replicas):
    group, rows, width = own.shape
    half = group // 2
    scale = 1.0 / replicas

    def kernel(table_ref, own_ref, *refs):
        halves, out = refs[:4], refs[4]
        out[...] = jnp.zeros(out.shape, BF16)
        me = lax.axis_index("dp")

        def step(j, _):
            for i in range(2):
                entry = table_ref[me * group + i * half + j]
                total = own_ref[i * half + j].astype(F32) + halves[i][j].astype(F32)
                total = total + halves[2 + i][j].astype(F32)
                column = pl.multiple_of((entry & 1) * width, width)
                out[entry >> 1, :, pl.ds(column, width)] = (total * scale).astype(BF16)
            return 0

        lax.fori_loop(0, half, step, 0, unroll=8)

    outs = [shape(devices, rows, slots * width)]
    args = [table, own, *near, *passed]
    return call(kernel, outs, [SMEM] + [VMEM] * 5, args, "mean")[0]


def precondition(grads, left, right):
    size = left.shape[1]

    def kernel(grads_ref, left_ref, right_ref, first, second, room, sem):
        def scaled(slot):
            grad = grads_ref[:, slot * size : (slot + 1) * size]
            part = jnp.dot(left_ref[slot], grad, preferred_element_type=F32).astype(BF16)
            direction = jnp.dot(part, right_ref[slot], preferred_element_type=F32)
            power = jnp.sum(direction * direction) * (1.0 / (size * size))
            return (direction * lax.rsqrt(power + EPS)).astype(BF16)

        room[...] = scaled(1)
        copy = pltpu.make_async_copy(room, second, sem)
        copy.start()
        first[...] = scaled(0)
        copy.wait()

    outs = [shape(size, size)] * 2
    scratch = [pltpu.VMEM((size, size), BF16), pltpu.SemaphoreType.DMA]
    args = [grads, left, right]
    return call(kernel, outs, [VMEM] * 3, args, "direction", scratch, [VMEM, HBM])


def pick_first(table, first, pieces, group):
    rows, width = pieces.shape[1:]
    half = (group - SECOND) // 2

    def kernel(table_ref, first_ref, pieces_ref, *outs):
        start = lax.axis_index("dp") * group

        def step(j, _):
            for i, out in enumerate(outs):
                block = first_ref[start + i * half + j]
                out[j] = pieces_ref[table_ref[start + block] >> 1]
            return 0

        lax.fori_loop(0, half, step, 0, unroll=4)

    return pl.pallas_call(
        kernel,
        out_shape=[shape(half, rows, width)] * 2,
        grid=(1,),
        in_specs=[SMEM, SMEM, pl.BlockSpec((pieces.shape[0], rows, width), lambda i: (0, 0, 0))],
        out_specs=[pl.BlockSpec((half, rows, width), lambda i: (0, 0, 0))] * 2,
        compiler_params=PARAMS,
        name="pick_first",
    )(table, first, pieces)


def pick_second(table, at, pieces):
    rows, width = pieces.shape[1:]

    def kernel(table_ref, at_ref, pieces_ref, out, sem):
        me = lax.axis_index("dp")
        for i in range(SECOND):
            owner = table_ref[at_ref[me * LIST + i]] >> 1
            pltpu.make_async_copy(pieces_ref.at[owner], out.at[i], sem).start()
        pltpu.make_async_copy(pieces_ref.at[pl.ds(0, SECOND)], out, sem).wait()

    outs = [shape(SECOND, rows, width)]
    scratch = [pltpu.SemaphoreType.DMA]
    args = [table, at, pieces]
    return call(kernel, outs, [SMEM, SMEM, HBM], args, "pick_second", scratch)[0]


def block_lists(table, group, replicas):
    def kernel(table_ref, first, at):
        for g in range(replicas):
            in_first = jnp.int32(0)
            in_second = jnp.int32(0)
            for j in range(group):
                odd = table_ref[g * group + j] & 1
                first[g * group + in_first] = j
                at[g * LIST + in_second] = g * group + j
                in_first = in_first + (1 - odd)
                in_second = in_second + odd

    outs = [shape(replicas * n, dtype=jnp.int32) for n in (group, LIST)]
    return call(kernel, outs, [SMEM], [table], "block_lists", out_specs=[SMEM, SMEM])


def lay(first, groups, halves, group, update_shape, update=None):
    half, rows, width = halves[0].shape
    given = 0 if update is None else 1

    def kernel(first_ref, *refs):
        refs = refs[given:]
        sources, (out, room, sems) = refs[:-3], refs[-3:]
        places = around()
        copies = []
        for k, at in enumerate(groups):
            g = places[at]

            def step(j, _, k=k, g=g):
                for i in range(2):
                    block = first_ref[g * group + i * half + j]
                    room[k * group + block] = sources[2 * k + i][j]
                return 0

            lax.fori_loop(0, half, step, 0, unroll=4)
            source = room.at[pl.ds(k * group, group)]
            copies.append(
                pltpu.make_async_copy(source, out.at[pl.ds(g * group, group)], sems.at[k])
            )
            copies[-1].start()
        for copy in copies:
            copy.wait()

    return pl.pallas_call(
        kernel,
        out_shape=shape(*update_shape),
        in_specs=[SMEM] + [HBM] * given + [VMEM] * len(halves),
        out_specs=HBM,
        scratch_shapes=[
            pltpu.VMEM((len(groups) * group, rows, width), BF16),
            pltpu.SemaphoreType.DMA((len(groups),)),
        ],
        input_output_aliases={1: 0} if given else {},
        compiler_params=PARAMS,
        name="lay",
    )(first, *([update] if given else []), *halves)


def lay_second(update, at, seconds):
    replicas = len(seconds)

    def kernel(at_ref, _, *refs):
        sources, (out, sems) = refs[:replicas], refs[replicas:]
        for k, g in enumerate(around()):
            for i in range(SECOND):
                pltpu.make_async_copy(
                    sources[k].at[i], out.at[at_ref[g * LIST + i]], sems.at[k]
                ).start()
        for k in range(replicas):
            pltpu.make_async_copy(sources[k], out.at[pl.ds(0, SECOND)], sems.at[k]).wait()

    return pl.pallas_call(
        kernel,
        out_shape=shape(*update.shape),
        in_specs=[SMEM, HBM] + [VMEM] * replicas,
        out_specs=HBM,
        scratch_shapes=[pltpu.SemaphoreType.DMA((replicas,))],
        input_output_aliases={1: 0},
        compiler_params=PARAMS,
        name="lay_second",
    )(at, update, *seconds)


def new_statistics(counts, grads, stats_left, stats_right, parts=2):
    slots, size = stats_left.shape[:2]
    tile = size // parts

    def kernel(counts_ref, grads_ref, left_ref, right_ref, new_left_ref, new_right_ref):
        live = counts_ref[0] > pl.program_id(0)
        for p in range(parts):

            @pl.when(pl.program_id(1) == p)
            def _(p=p):
                grad = grads_ref[...]
                span = slice(p * tile, (p + 1) * tile)
                gram_left = lax.dot_general(
                    grad[span], grad, (((1,), (1,)), ((), ())), preferred_element_type=F32
                )
                gram_right = lax.dot_general(
                    grad[:, span], grad, (((0,), (0,)), ((), ())), preferred_element_type=F32
                )
                old_left, old_right = left_ref[0], right_ref[0]
                new_left_ref[0] = jnp.where(
                    live, BETA * old_left + (1.0 - BETA) * gram_left, old_left
                )
                new_right_ref[0] = jnp.where(
                    live, BETA * old_right + (1.0 - BETA) * gram_right, old_right
                )

    block = pl.BlockSpec((size, size), lambda s, t: (0, s))
    part = pl.BlockSpec((1, tile, size), lambda s, t: (s, t, 0))
    return pl.pallas_call(
        kernel,
        out_shape=[shape(*stats_left.shape, dtype=F32)] * 2,
        grid=(slots, parts),
        in_specs=[SMEM, block, part, part],
        out_specs=[part, part],
        compiler_params=PARAMS,
        cost_estimate=pl.CostEstimate(
            flops=8 * size**3, bytes_accessed=16 * 2 * size * size, transcendentals=0
        ),
        name="statistics",
    )(counts, grads, stats_left, stats_right)


def local(grads, stats_left, stats_right, precond_left, precond_right, owner_table, block_counts):
    devices = lax.axis_size("fsdp")
    replicas = lax.axis_size("dp")
    blocks, rows, width = grads.shape[1:]
    slots, size = stats_left.shape[:2]
    group = blocks // replicas
    mine = pltpu.with_memory_space_constraint(grads[0], pltpu.HBM)
    send = lambda pieces, pairs: lax.ppermute(pieces, "dp", pairs)
    exchange = lambda pieces: lax.all_to_all(pieces, "fsdp", 0, 0, tiled=True)

    far_next, far_last = first_sends(mine, group, True)
    near_next, near_last = first_sends(mine, group, False)
    own, *kept_halves = kept(mine, group)
    arrived = [send(far_next, NEXT), send(far_last, LAST)]
    near = [send(near_next, NEXT), send(near_last, LAST)]
    first, at = block_lists(owner_table, group, replicas)
    kept_halves, first, at = lax.optimization_barrier((kept_halves, first, at))
    low, high = partial_sums(kept_halves, arrived)
    passed = [send(low, LAST), send(high, NEXT)]
    outgoing = place_mean(owner_table, own, near, passed, devices, slots, replicas)
    owned = exchange(outgoing).reshape(size, slots * width)
    scaled_first, scaled_second = precondition(owned, precond_left, precond_right)
    first_back = exchange(scaled_first.reshape(devices, rows, width))
    scaled_second, first_back = lax.optimization_barrier((scaled_second, first_back))
    second_back = exchange(scaled_second.reshape(devices, rows, width))

    low, high = pick_first(owner_table, first, first_back, group)
    last_low, next_high = send(low, LAST), send(high, NEXT)
    next_low, last_high = send(low, NEXT), send(high, LAST)
    owned, _ = lax.optimization_barrier((owned, low))
    old_left, old_right = (
        pltpu.with_memory_space_constraint(old, pltpu.HBM) for old in (stats_left, stats_right)
    )
    stats = new_statistics(
        block_counts.reshape(1), owned, old_left, old_right
    )
    last_low, next_high, stats = lax.optimization_barrier((last_low, next_high, stats))
    across = [send(last_low, NEXT), send(next_high, LAST)]
    second_rows = pick_second(owner_table, at, second_back)
    seconds = [second_rows] + [send(second_rows, p) for p in (NEXT, LAST, OPPOSITE)]
    near_rows = [low, high, next_low, next_high, last_low, last_high]
    update = lay(first, (0, 1, 2), near_rows, group, mine.shape)
    update = lay(first, (3,), across, group, mine.shape, update)
    update = lay_second(update, at, seconds)
    return (*stats, update)


def solution(mesh):
    in_specs = (
        P("dp", None, "fsdp", None),
        P(("dp", "fsdp"), None, None),
        P(("dp", "fsdp"), None, None),
        P(("dp", "fsdp"), None, None),
        P(("dp", "fsdp"), None, None),
        P(),
        P("dp", "fsdp"),
    )
    out_specs = (
        P(("dp", "fsdp"), None, None),
        P(("dp", "fsdp"), None, None),
        P(None, "fsdp", None),
    )
    return jax.shard_map(local, mesh=mesh, in_specs=in_specs, out_specs=out_specs, check_vma=False)
```

```python
import jax
import jax.numpy as jnp
from jax import lax
from jax.experimental import pallas as pl
from jax.experimental.pallas import tpu as pltpu
from jax.sharding import PartitionSpec as P

BETA = 0.9
EPS = 1e-06
BF16 = jnp.bfloat16
F32 = jnp.float32

NEXT = [(i, i ^ 1) for i in range(4)]
LAST = [(i, 3 - i) for i in range(4)]
OPPOSITE = [(i, i ^ 2) for i in range(4)]
SECOND = 8
LIST = 16

VMEM = pl.BlockSpec(memory_space=pltpu.VMEM)
SMEM = pl.BlockSpec(memory_space=pltpu.SMEM)
HBM = pl.BlockSpec(memory_space=pltpu.HBM)
PARAMS = pltpu.CompilerParams(vmem_limit_bytes=16 * 1024 * 1024)


def shape(*dims, dtype=BF16):
    return jax.ShapeDtypeStruct(dims, dtype)


def call(kernel, outs, in_specs, args, name, scratch=(), out_specs=None):
    return pl.pallas_call(
        kernel,
        out_shape=outs,
        in_specs=in_specs,
        out_specs=[VMEM] * len(outs) if out_specs is None else out_specs,
        scratch_shapes=scratch,
        compiler_params=PARAMS,
        name=name,
    )(*args)


def around():
    me = lax.axis_index("dp")
    return me, me ^ 1, 3 - me, me ^ 2


def copy_all(pairs, sems):
    copies = [
        pltpu.make_async_copy(source, target, sems.at[i])
        for i, (source, target) in enumerate(pairs)
    ]
    for copy in copies:
        copy.start()
    for copy in copies:
        copy.wait()


def first_sends(grads, group, far):
    rows, width = grads.shape[1:]
    half = group // 2

    def kernel(grads_ref, to_next, to_last, sems):
        _, after, before, opposite = around()
        groups = (opposite, opposite) if far else (after, before)
        pairs = [
            (grads_ref.at[pl.ds(g * group + i * half, half)], out)
            for i, (g, out) in enumerate(zip(groups, (to_next, to_last)))
        ]
        copy_all(pairs, sems)

    outs = [shape(half, rows, width)] * 2
    name = "far_sends" if far else "near_sends"
    return call(kernel, outs, [HBM], [grads], name, [pltpu.SemaphoreType.DMA((2,))])


def kept(grads, group):
    rows, width = grads.shape[1:]
    half = group // 2

    def kernel(grads_ref, own, low, high, sems):
        me, after, before, _ = around()
        part = lambda g, i, count: grads_ref.at[pl.ds(g * group + i * half, count)]
        pairs = [(part(me, 0, group), own), (part(before, 0, half), low), (part(after, 1, half), high)]
        copy_all(pairs, sems)

    outs = [shape(group, rows, width)] + [shape(half, rows, width)] * 2
    return call(kernel, outs, [HBM], [grads], "kept", [pltpu.SemaphoreType.DMA((3,))])


def partial_sums(kept_halves, arrived):
    dims = arrived[0].shape

    def kernel(low_kept, high_kept, low_got, high_got, low, high):
        def step(j, _):
            low[j] = (low_kept[j].astype(F32) + low_got[j].astype(F32)).astype(BF16)
            high[j] = (high_kept[j].astype(F32) + high_got[j].astype(F32)).astype(BF16)
            return 0

        lax.fori_loop(0, dims[0], step, 0, unroll=8)

    return call(kernel, [shape(*dims)] * 2, [VMEM] * 4, [*kept_halves, *arrived], "partial")


def place_mean(table, own, near, passed, devices, slots, replicas):
    group, rows, width = own.shape
    half = group // 2
    scale = 1.0 / replicas

    def kernel(table_ref, own_ref, *refs):
        halves, out = refs[:4], refs[4]
        out[...] = jnp.zeros(out.shape, BF16)
        me = lax.axis_index("dp")

        def step(j, _):
            for i in range(2):
                entry = table_ref[me * group + i * half + j]
                total = own_ref[i * half + j].astype(F32) + halves[i][j].astype(F32)
                total = total + halves[2 + i][j].astype(F32)
                column = pl.multiple_of((entry & 1) * width, width)
                out[entry >> 1, :, pl.ds(column, width)] = (total * scale).astype(BF16)
            return 0

        lax.fori_loop(0, half, step, 0, unroll=8)

    outs = [shape(devices, rows, slots * width)]
    args = [table, own, *near, *passed]
    return call(kernel, outs, [SMEM] + [VMEM] * 5, args, "mean")[0]


def precondition(grads, left, right):
    size = left.shape[1]

    def kernel(grads_ref, left_ref, right_ref, first, second, room, sem):
        def direction(slot):
            grad = grads_ref[:, slot * size : (slot + 1) * size]
            part = jnp.dot(left_ref[slot], grad, preferred_element_type=F32).astype(BF16)
            return jnp.dot(part, right_ref[slot], preferred_element_type=F32)

        def scaled(value):
            power = jnp.sum(value * value) * (1.0 / (size * size))
            return (value * lax.rsqrt(power + EPS)).astype(BF16)

        of_second, of_first = direction(1), direction(0)
        room[...] = scaled(of_second)
        copy = pltpu.make_async_copy(room, second, sem)
        copy.start()
        first[...] = scaled(of_first)
        copy.wait()

    outs = [shape(size, size)] * 2
    scratch = [pltpu.VMEM((size, size), BF16), pltpu.SemaphoreType.DMA]
    args = [grads, left, right]
    return call(kernel, outs, [VMEM] * 3, args, "direction", scratch, [VMEM, HBM])


def pick_first(table, first, pieces, group):
    rows, width = pieces.shape[1:]
    half = (group - SECOND) // 2

    def kernel(table_ref, first_ref, pieces_ref, *outs):
        start = lax.axis_index("dp") * group

        def step(j, _):
            for i, out in enumerate(outs):
                block = first_ref[start + i * half + j]
                out[j] = pieces_ref[table_ref[start + block] >> 1]
            return 0

        lax.fori_loop(0, half, step, 0, unroll=4)

    return pl.pallas_call(
        kernel,
        out_shape=[shape(half, rows, width)] * 2,
        grid=(1,),
        in_specs=[SMEM, SMEM, pl.BlockSpec((pieces.shape[0], rows, width), lambda i: (0, 0, 0))],
        out_specs=[pl.BlockSpec((half, rows, width), lambda i: (0, 0, 0))] * 2,
        compiler_params=PARAMS,
        name="pick_first",
    )(table, first, pieces)


def pick_second(table, at, pieces):
    rows, width = pieces.shape[1:]

    def kernel(table_ref, at_ref, pieces_ref, out, sem):
        me = lax.axis_index("dp")
        for i in range(SECOND):
            owner = table_ref[at_ref[me * LIST + i]] >> 1
            pltpu.make_async_copy(pieces_ref.at[owner], out.at[i], sem).start()
        pltpu.make_async_copy(pieces_ref.at[pl.ds(0, SECOND)], out, sem).wait()

    outs = [shape(SECOND, rows, width)]
    scratch = [pltpu.SemaphoreType.DMA]
    args = [table, at, pieces]
    return call(kernel, outs, [SMEM, SMEM, HBM], args, "pick_second", scratch)[0]


def block_lists(table, group, replicas):
    def kernel(table_ref, first, at):
        for g in range(replicas):
            in_first = jnp.int32(0)
            in_second = jnp.int32(0)
            for j in range(group):
                odd = table_ref[g * group + j] & 1
                first[g * group + in_first] = j
                at[g * LIST + in_second] = g * group + j
                in_first = in_first + (1 - odd)
                in_second = in_second + odd

    outs = [shape(replicas * n, dtype=jnp.int32) for n in (group, LIST)]
    return call(kernel, outs, [SMEM], [table], "block_lists", out_specs=[SMEM, SMEM])


def lay(first, groups, halves, group, update_shape, update=None):
    half, rows, width = halves[0].shape
    given = 0 if update is None else 1

    def kernel(first_ref, *refs):
        refs = refs[given:]
        sources, (out, room, sems) = refs[:-3], refs[-3:]
        places = around()
        copies = []
        for k, at in enumerate(groups):
            g = places[at]

            def step(j, _, k=k, g=g):
                for i in range(2):
                    block = first_ref[g * group + i * half + j]
                    room[k * group + block] = sources[2 * k + i][j]
                return 0

            lax.fori_loop(0, half, step, 0, unroll=4)
            source = room.at[pl.ds(k * group, group)]
            copies.append(
                pltpu.make_async_copy(source, out.at[pl.ds(g * group, group)], sems.at[k])
            )
            copies[-1].start()
        for copy in copies:
            copy.wait()

    return pl.pallas_call(
        kernel,
        out_shape=shape(*update_shape),
        in_specs=[SMEM] + [HBM] * given + [VMEM] * len(halves),
        out_specs=HBM,
        scratch_shapes=[
            pltpu.VMEM((len(groups) * group, rows, width), BF16),
            pltpu.SemaphoreType.DMA((len(groups),)),
        ],
        input_output_aliases={1: 0} if given else {},
        compiler_params=PARAMS,
        name="lay",
    )(first, *([update] if given else []), *halves)


def lay_second(update, at, seconds):
    replicas = len(seconds)

    def kernel(at_ref, _, *refs):
        sources, (out, sems) = refs[:replicas], refs[replicas:]
        for k, g in enumerate(around()):
            for i in range(SECOND):
                pltpu.make_async_copy(
                    sources[k].at[i], out.at[at_ref[g * LIST + i]], sems.at[k]
                ).start()
        for k in range(replicas):
            pltpu.make_async_copy(sources[k], out.at[pl.ds(0, SECOND)], sems.at[k]).wait()

    return pl.pallas_call(
        kernel,
        out_shape=shape(*update.shape),
        in_specs=[SMEM, HBM] + [VMEM] * replicas,
        out_specs=HBM,
        scratch_shapes=[pltpu.SemaphoreType.DMA((replicas,))],
        input_output_aliases={1: 0},
        compiler_params=PARAMS,
        name="lay_second",
    )(at, update, *seconds)


def new_statistics(counts, grads, stats_left, stats_right, parts=2):
    slots, size = stats_left.shape[:2]
    tile = size // parts

    def kernel(counts_ref, grads_ref, left_ref, right_ref, new_left_ref, new_right_ref):
        live = counts_ref[0] > pl.program_id(0)
        for p in range(parts):

            @pl.when(pl.program_id(1) == p)
            def _(p=p):
                grad = grads_ref[...]
                span = slice(p * tile, (p + 1) * tile)
                gram_left = lax.dot_general(
                    grad[span], grad, (((1,), (1,)), ((), ())), preferred_element_type=F32
                )
                gram_right = lax.dot_general(
                    grad[:, span], grad, (((0,), (0,)), ((), ())), preferred_element_type=F32
                )
                old_left, old_right = left_ref[0], right_ref[0]
                new_left_ref[0] = jnp.where(
                    live, BETA * old_left + (1.0 - BETA) * gram_left, old_left
                )
                new_right_ref[0] = jnp.where(
                    live, BETA * old_right + (1.0 - BETA) * gram_right, old_right
                )

    block = pl.BlockSpec((size, size), lambda s, t: (0, s))
    part = pl.BlockSpec((1, tile, size), lambda s, t: (s, t, 0))
    return pl.pallas_call(
        kernel,
        out_shape=[shape(*stats_left.shape, dtype=F32)] * 2,
        grid=(slots, parts),
        in_specs=[SMEM, block, part, part],
        out_specs=[part, part],
        compiler_params=PARAMS,
        cost_estimate=pl.CostEstimate(
            flops=8 * size**3, bytes_accessed=16 * 2 * size * size, transcendentals=0
        ),
        name="statistics",
    )(counts, grads, stats_left, stats_right)


def local(grads, stats_left, stats_right, precond_left, precond_right, owner_table, block_counts):
    devices = lax.axis_size("fsdp")
    replicas = lax.axis_size("dp")
    blocks, rows, width = grads.shape[1:]
    slots, size = stats_left.shape[:2]
    group = blocks // replicas
    mine = pltpu.with_memory_space_constraint(grads[0], pltpu.HBM)
    send = lambda pieces, pairs: lax.ppermute(pieces, "dp", pairs)
    exchange = lambda pieces: lax.all_to_all(pieces, "fsdp", 0, 0, tiled=True)

    far_next, far_last = first_sends(mine, group, True)
    near_next, near_last = first_sends(mine, group, False)
    own, *kept_halves = kept(mine, group)
    arrived = [send(far_next, NEXT), send(far_last, LAST)]
    near = [send(near_next, NEXT), send(near_last, LAST)]
    first, at = block_lists(owner_table, group, replicas)
    kept_halves, first, at = lax.optimization_barrier((kept_halves, first, at))
    low, high = partial_sums(kept_halves, arrived)
    passed = [send(low, LAST), send(high, NEXT)]
    outgoing = place_mean(owner_table, own, near, passed, devices, slots, replicas)
    owned = exchange(outgoing).reshape(size, slots * width)
    scaled_first, scaled_second = precondition(owned, precond_left, precond_right)
    first_back = exchange(scaled_first.reshape(devices, rows, width))
    scaled_second, first_back = lax.optimization_barrier((scaled_second, first_back))
    second_back = exchange(scaled_second.reshape(devices, rows, width))

    low, high = pick_first(owner_table, first, first_back, group)
    last_low, next_high = send(low, LAST), send(high, NEXT)
    next_low, last_high = send(low, NEXT), send(high, LAST)
    owned, _ = lax.optimization_barrier((owned, low))
    old_left, old_right = (
        pltpu.with_memory_space_constraint(old, pltpu.HBM) for old in (stats_left, stats_right)
    )
    stats = new_statistics(
        block_counts.reshape(1), owned, old_left, old_right
    )
    last_low, next_high, stats = lax.optimization_barrier((last_low, next_high, stats))
    across = [send(last_low, NEXT), send(next_high, LAST)]
    second_rows = pick_second(owner_table, at, second_back)
    seconds = [second_rows] + [send(second_rows, p) for p in (NEXT, LAST, OPPOSITE)]
    near_rows = [low, high, next_low, next_high, last_low, last_high]
    update = lay(first, (0, 1, 2), near_rows, group, mine.shape)
    update = lay(first, (3,), across, group, mine.shape, update)
    update = lay_second(update, at, seconds)
    return (*stats, update)


def solution(mesh):
    in_specs = (
        P("dp", None, "fsdp", None),
        P(("dp", "fsdp"), None, None),
        P(("dp", "fsdp"), None, None),
        P(("dp", "fsdp"), None, None),
        P(("dp", "fsdp"), None, None),
        P(),
        P("dp", "fsdp"),
    )
    out_specs = (
        P(("dp", "fsdp"), None, None),
        P(("dp", "fsdp"), None, None),
        P(None, "fsdp", None),
    )
    return jax.shard_map(local, mesh=mesh, in_specs=in_specs, out_specs=out_specs, check_vma=False)
```
